32 devices in a mesh: pipe: 2 (over x), dp: 4 (over y, core), expert: 4 (over z).
Axes of the slice: x: 2, y: 2, z: 4, core: 2. Of those that a mesh axis runs over, the one named last changes fastest.
Arguments:
- tokens: bfloat16 [512, 6144], P('expert', 'dp'), may hold values from -6 to 6
- expert_ids: int32 [512, 2], P('expert'), may hold values from 0 to 7, all different within a row; in each aligned block of 128 rows (0 to 127, 128 to 255, ...) at most 34 rows name the same one
- gates: float32 [512, 2], P('expert'), may hold values from 0.1 to 1
- w_up: bfloat16 [16, 6144, 4096], P('expert', 'dp', 'pipe'), may hold values from -0.078125 to 0.078125
- w_down: bfloat16 [16, 4096, 6144], P('expert', 'pipe', 'dp'), may hold values from -0.0625 to 0.0625
- cotangent: bfloat16 [512, 6144], P('expert', 'dp'), may hold values from -6 to 6
Outputs:
- output: bfloat16 [512, 6144], P('expert', ('dp', 'pipe'))
- token_grad: bfloat16 [512, 6144], P('expert', ('dp', 'pipe'))
- up_grad: bfloat16 [16, 6144, 4096], P('expert', 'dp', 'pipe')
- down_grad: bfloat16 [16, 4096, 6144], P('expert', 'pipe', 'dp')
The draws below stay inside these ranges and needn't reach their ends.
Inputs may be any that keep to these rules, and one draw needn't show every extreme that they name: `expert_ids`: the two ids of a token differ. Among the 128 rows of one index of the expert axis (aligned blocks of rows), no expert is named by more than 34 rows, a bound that some block reaches.
All inputs are finite; a program needn't handle non-finite values.
Results may differ from the reference program's by a relative error of at most 0.027.
Values may be sent and summed in bfloat16 or wider, within the bound.
A program may use at most 192 MiB of HBM per device.

```python
import math
import jax
import jax.numpy as jnp
import numpy as np
from jax import lax

D = 6144
FF = 8192
E = 8
TOP = 2
TOK_DEV = 128
CAP = 34
TOKENS = 512
N_DP = 4
N_EXPERT = 4


def block_levels(own_key, dims, cuts, low, high):
    factor_of, own = 1.0, jax.random.fold_in(own_key, 6)
    for axis_at, shards_of in cuts:
        steps = jnp.exp(jax.random.uniform(jax.random.fold_in(own, axis_at), (shards_of,), jnp.float32, low / len(cuts), high / len(cuts)))
        factor_of = factor_of * jnp.repeat(steps, dims[axis_at] // shards_of).reshape([-1 if axis == axis_at else 1 for axis in range(len(dims))])
    return factor_of


def shared_out(rng, own, number, rows, count, top, limit, skew):
    order = jax.random.permutation(rng, count)
    heavy_load, common = shares(count, rows * top, limit, skew, True), shares(count, rows * top, limit, skew, False)
    places = jnp.arange(count)

    def named(tallies, turn):
        used = int((tallies > 0).sum())
        fixed = max(1, used // 4)
        shifted = fixed + (places - fixed + turn * (used - fixed)) % max(1, count - fixed)
        return jnp.zeros((count,), jnp.int32).at[order[jnp.where(places < fixed, places, shifted)]].set(jnp.asarray(tallies, jnp.int32))

    tallies = jnp.where(number % 4 == 0, named(heavy_load, number // 4), named(common, number - number // 4 - 1))
    mixed = jax.random.permutation(jax.random.fold_in(own, 3), count)
    giver, taker = mixed[0:count // 2 * 2:2], mixed[1:count // 2 * 2:2]
    room = jnp.minimum(tallies[giver] - 1, limit - tallies[taker]) // 2
    room = jnp.where((giver == order[0]) | (taker == order[0]) | (tallies[taker] == 0), 0, jnp.maximum(room, 0))
    shifted = jax.random.randint(jax.random.fold_in(own, 4), (count // 2,), 0, 1 << 20) % (room + 1)
    tallies = tallies.at[giver].add(-shifted).at[taker].add(shifted)
    labels = jnp.searchsorted(jnp.cumsum(tallies), jnp.arange(rows * top), side="right").astype(jnp.int32)
    listing = labels.reshape(top, rows).T
    listing = listing[jax.random.permutation(jax.random.fold_in(own, 1), rows)]
    turn = jax.random.randint(jax.random.fold_in(own, 2), (rows, 1), 0, top)
    return jnp.take_along_axis(listing, (jnp.arange(top)[None, :] + turn) % top, axis=1)


def shares(amount, total, most, skew, full):
    loads = [(1 << 20) // math.isqrt(standing ** skew) + 1 for standing in range(1, amount + 1)]
    largest = most if full else min(most, max(-(-total // amount), total * loads[0] // sum(loads)))
    least = 1 if total - largest >= amount - 1 else 0
    given, spare = [largest] + [least] * (amount - 1), total - largest - least * (amount - 1)
    while spare > 0:
        free = [i for i in range(1, amount) if given[i] < largest] or [i for i in range(1, amount) if given[i] < most]
        whole, left = sum([loads[i] for i in free]), spare
        for i in free:
            addition = min(most - given[i], max(1, left * loads[i] // whole), spare)
            given[i] = given[i] + addition
            spare = spare - addition
    return np.array(given)


def bell_draw(key, dims, deviation, most, cuts=(), held_as=jnp.bfloat16):
    drawn = deviation * jax.random.normal(key, dims, jnp.float32)
    if cuts:
        drawn = drawn * block_levels(key, dims, cuts, -0.22, 0.18)
    return jnp.clip(drawn, -most, most).astype(held_as)


def setup_inputs(seed: int = 0) -> dict:
    seeds = jax.random.split(jax.random.key(seed), 7)
    tokens = bell_draw(seeds[0], (TOKENS, D), 1.0, 6.0, ((0, 4), (1, 4)))
    expert_ids_keys = jax.random.split(jax.random.fold_in(seeds[1], 1), TOKENS // TOK_DEV)
    expert_ids_turns = jax.random.permutation(jax.random.fold_in(seeds[1], 3), TOKENS // TOK_DEV)
    expert_ids = jax.vmap(lambda own, number: shared_out(jax.random.fold_in(seeds[1], 2), own, number, TOK_DEV, E, TOP, CAP, 2))(expert_ids_keys, expert_ids_turns).reshape((TOKENS, TOP))
    gates = jnp.clip(0.1 + 0.9 * jax.random.uniform(seeds[2], (TOKENS, TOP), jnp.float32) ** block_levels(seeds[2], (TOKENS, TOP), ((0, 4),), -0.2, 0.2), 0.1, 1.0)
    w_up = bell_draw(seeds[3], (2 * E, D, FF // 2), D ** -0.5, 0.078125, ((0, 4), (1, 4), (2, 2)))
    w_down = bell_draw(seeds[4], (2 * E, FF // 2, D), FF ** -0.5, 0.0625, ((0, 4), (1, 2), (2, 4)))
    cotangent = bell_draw(seeds[5], (TOKENS, D), 1.0, 6.0, ((0, 4), (1, 4)))
    return {"tokens": tokens, "expert_ids": expert_ids, "gates": gates, "w_up": w_up, "w_down": w_down, "cotangent": cotangent}


def silu_slope(pre):
    sigma = jax.nn.sigmoid(pre)
    return sigma * (1.0 + pre * (1.0 - sigma))


def reference(tokens, expert_ids, gates, w_up, w_down, cotangent):
    half = FF // 2
    rows = N_EXPERT * CAP
    block = D // N_DP
    out_total = jnp.zeros((TOKENS, D), jnp.float32)
    back_total = jnp.zeros((TOKENS, D), jnp.float32)
    up_pieces = []
    down_pieces = []
    for expert in range(E):
        up_full = jnp.concatenate([w_up[2 * expert], w_up[2 * expert + 1]], axis=1)
        down_full = jnp.concatenate([w_down[2 * expert], w_down[2 * expert + 1]], axis=0)
        weight_all = jnp.sum(jnp.where(expert_ids == expert, gates, jnp.float32(0.0)), axis=1)
        missing = 1 - jnp.any(expert_ids == expert, axis=1).astype(jnp.int32)
        picked = jnp.argsort(missing, stable=True)[:rows].astype(jnp.int32)
        mine = tokens[picked]
        weight = weight_all[picked]
        cot_rows = cotangent[picked]
        pre = jnp.dot(mine, up_full, preferred_element_type=jnp.float32)
        hidden = jax.nn.silu(pre).astype(jnp.bfloat16)
        result = jnp.dot(hidden, down_full, preferred_element_type=jnp.float32)
        out_total = out_total.at[picked].add(weight[:, None] * result)
        grad_rows = (weight[:, None] * cot_rows.astype(jnp.float32)).astype(jnp.bfloat16)
        grad_hidden = jnp.zeros((rows, FF), jnp.float32)
        for part in range(N_DP):
            piece = jnp.dot(grad_rows[:, part * block:(part + 1) * block],
                            down_full[:, part * block:(part + 1) * block].T,
                            preferred_element_type=jnp.float32).astype(jnp.bfloat16)
            piece = lax.optimization_barrier(piece)
            grad_hidden = grad_hidden + piece.astype(jnp.float32)
        grad_pre = (grad_hidden * silu_slope(pre)).astype(jnp.bfloat16)
        down_grad = jnp.dot(hidden.T, grad_rows, preferred_element_type=jnp.float32).astype(jnp.bfloat16)
        up_grad = jnp.dot(mine.T, grad_pre, preferred_element_type=jnp.float32).astype(jnp.bfloat16)
        back_total = back_total.at[picked].add(jnp.dot(grad_pre, up_full.T, preferred_element_type=jnp.float32))
        up_pieces = up_pieces + [up_grad[:, :half], up_grad[:, half:]]
        down_pieces = down_pieces + [down_grad[:half], down_grad[half:]]
    return (out_total.astype(jnp.bfloat16), back_total.astype(jnp.bfloat16),
            jnp.stack(up_pieces), jnp.stack(down_pieces))
```

```python
import jax
import jax.numpy as jnp
from jax import lax
from jax.sharding import PartitionSpec as P

CAP = 34
BF = jnp.bfloat16
F32 = jnp.float32


def silu_slope(pre):
    sigma = jax.nn.sigmoid(pre)
    return sigma * (1.0 + pre * (1.0 - sigma))


def swap(value, axis, bit):
    count = lax.axis_size(axis)
    return lax.ppermute(value, axis, [(i, i ^ bit) for i in range(count)])


def pick(value, index, axis):
    return lax.dynamic_index_in_dim(value, index, axis, keepdims=False)


def sum_over_features(part):
    count = lax.axis_size("dp")
    pairs, rows, hidden = part.shape
    if count != 4 or pairs % 4:
        return lax.psum_scatter(part, "dp", scatter_dimension=2, tiled=True).astype(F32)
    me = lax.axis_index("dp")
    core, chip = me % 2, me // 2
    cut = part.reshape(2, 2, pairs // 4, rows, hidden)
    other = swap(pick(cut, 1 - core, 1), "dp", 1)
    near = (pick(cut, core, 1).astype(F32) + other.astype(F32)).astype(BF)
    far = swap(pick(near, 1 - chip, 0), "dp", 2)
    return pick(near, chip, 0).astype(F32) + far.astype(F32)


def share_of_features(value, pairs):
    if lax.axis_size("dp") != 4 or pairs % 4:
        return lax.all_gather(value, "dp", axis=2, tiled=True)
    return lax.all_gather(value, "dp", axis=0, tiled=True)


def sum_over_hidden(part):
    count = lax.axis_size("pipe")
    part = part.astype(BF)
    if count != 2:
        return lax.psum_scatter(part, "pipe", scatter_dimension=2, tiled=True).astype(F32)
    me = lax.axis_index("pipe")
    width = part.shape[2] // 2
    sent = swap(lax.dynamic_slice_in_dim(part, (1 - me) * width, width, 2), "pipe", 1)
    return lax.dynamic_slice_in_dim(part, me * width, width, 2).astype(F32) + sent.astype(F32)


def on_device(tokens, expert_ids, gates, w_up, w_down, cotangent):
    groups = lax.axis_size("expert")
    pairs, features, hidden_width = w_up.shape
    halves = 2 if pairs % 2 == 0 else 1
    sets = pairs // halves
    rows = groups * CAP
    own = tokens.shape[0]
    count = groups * own

    meta = jnp.concatenate([expert_ids.astype(F32).T, gates.T], axis=0)
    meta = lax.all_gather(meta, "expert", axis=1, tiled=True)
    all_tokens = lax.all_gather(tokens, "expert", axis=0, tiled=True)
    all_cotangent = lax.all_gather(cotangent, "expert", axis=0, tiled=True)

    pair_ids = lax.axis_index("expert") * pairs + jnp.arange(pairs, dtype=jnp.int32)
    wanted = (pair_ids // 2).astype(F32)[:, None]
    first, second = meta[0:1] == wanted, meta[1:2] == wanted
    chosen = first | second
    weight = jnp.where(first, meta[2:3], 0.0) + jnp.where(second, meta[3:4], 0.0)
    before = jnp.arange(count)[:, None] < jnp.arange(count)[None, :]
    position = jnp.dot(chosen.astype(BF), before.astype(BF), preferred_element_type=F32)
    position = jnp.where(chosen, position, -1.0)
    slots = jnp.arange(rows, dtype=jnp.int32).astype(F32)[None, :, None]
    match = position[:, None, :] == slots
    routing = match.astype(BF).reshape(pairs * rows, count)
    row_weight = jnp.sum(jnp.where(match, weight[:, None, :], 0.0), axis=2)
    set_routing = match[::halves].astype(BF).reshape(sets * rows, count)
    set_weight = row_weight[::halves]

    arrived = jnp.dot(routing, all_tokens, preferred_element_type=F32)
    arrived = arrived.astype(BF).reshape(pairs, rows, features)
    pre_part = jnp.einsum("pcd,pdh->pch", arrived, w_up, preferred_element_type=F32).astype(BF)
    pre_share = sum_over_features(pre_part)

    grad_rows = jnp.dot(routing, all_cotangent, preferred_element_type=F32)
    grad_rows = (grad_rows.reshape(pairs, rows, features) * row_weight[:, :, None]).astype(BF)
    grad_part = jnp.einsum("pcd,phd->pch", grad_rows, w_down, preferred_element_type=F32).astype(BF)

    hidden = share_of_features(jax.nn.silu(pre_share).astype(BF), pairs)
    grad_share = sum_over_features(grad_part)
    grad_pre = share_of_features((grad_share * silu_slope(pre_share)).astype(BF), pairs)

    def by_set(value):
        return value.reshape((sets, halves) + value.shape[1:])

    out_part = jnp.einsum("rhck,rhkd->rcd", by_set(hidden), by_set(w_down), preferred_element_type=F32)
    out_rows = sum_over_hidden(out_part)
    back_part = jnp.einsum("rhck,rhdk->rcd", by_set(grad_pre), by_set(w_up), preferred_element_type=F32)
    back_rows = sum_over_hidden(back_part)

    def home(value):
        flat = value.astype(BF).reshape(sets * rows, value.shape[2])
        placed = lax.dot_general(
            set_routing, flat, (((0,), (0,)), ((), ())), preferred_element_type=F32
        )
        return lax.psum_scatter(placed.astype(BF), "expert", scatter_dimension=0, tiled=True)

    output = home(out_rows * set_weight[:, :, None])
    token_grad = home(back_rows)
    down_grad = jnp.einsum("pch,pcd->phd", hidden, grad_rows, preferred_element_type=F32).astype(BF)
    up_grad = jnp.einsum("pcd,pch->pdh", arrived, grad_pre, preferred_element_type=F32).astype(BF)
    return (output, token_grad, up_grad, down_grad)


def solution(mesh):
    return jax.shard_map(
        on_device,
        mesh=mesh,
        in_specs=(
            P("expert", "dp"),
            P("expert", None),
            P("expert", None),
            P("expert", "dp", "pipe"),
            P("expert", "pipe", "dp"),
            P("expert", "dp"),
        ),
        out_specs=(
            P("expert", ("dp", "pipe")),
            P("expert", ("dp", "pipe")),
            P("expert", "dp", "pipe"),
            P("expert", "pipe", "dp"),
        ),
        check_vma=False,
    )
```

```python
import jax
import jax.numpy as jnp
from jax import lax
from jax.sharding import PartitionSpec as P

CAP = 34
BF = jnp.bfloat16
F32 = jnp.float32


def silu_slope(pre):
    sigma = jax.nn.sigmoid(pre)
    return sigma * (1.0 + pre * (1.0 - sigma))


def swap(value, axis, bit):
    count = lax.axis_size(axis)
    return lax.ppermute(value, axis, [(i, i ^ bit) for i in range(count)])


def pick(value, index, axis):
    return lax.dynamic_index_in_dim(value, index, axis, keepdims=False)


def near_sum(part):
    count = lax.axis_size("dp")
    pairs, rows, hidden = part.shape
    if count != 4 or pairs % 4:
        return part
    core = lax.axis_index("dp") % 2
    cut = part.reshape(2, 2, pairs // 4, rows, hidden)
    other = swap(pick(cut, 1 - core, 1), "dp", 1)
    return (pick(cut, core, 1).astype(F32) + other.astype(F32)).astype(BF)


def far_sum(near):
    if near.ndim == 3:
        return lax.psum_scatter(near, "dp", scatter_dimension=2, tiled=True).astype(F32)
    chip = lax.axis_index("dp") // 2
    far = swap(pick(near, 1 - chip, 0), "dp", 2)
    return pick(near, chip, 0).astype(F32) + far.astype(F32)


def in_order(mine, other, index):
    first = jnp.where(index == 0, mine, other)
    second = jnp.where(index == 0, other, mine)
    return first, second


def share_of_features(value, pairs):
    if lax.axis_size("dp") != 4 or pairs % 4:
        return lax.all_gather(value, "dp", axis=2, tiled=True)
    me = lax.axis_index("dp")
    core, chip = me % 2, me // 2
    near = swap(value, "dp", 1)
    far = swap(value, "dp", 2)
    far_near = swap(far, "dp", 1)
    low, high = in_order(value, near, core)
    far_low, far_high = in_order(far, far_near, core)
    a0, a1 = in_order(low, far_low, chip)
    b0, b1 = in_order(high, far_high, chip)
    return jnp.concatenate([a0, b0, a1, b1], axis=0)


def sum_over_hidden(part):
    count = lax.axis_size("pipe")
    part = part.astype(BF)
    if count != 2:
        return lax.psum_scatter(part, "pipe", scatter_dimension=2, tiled=True).astype(F32)
    me = lax.axis_index("pipe")
    width = part.shape[2] // 2
    sent = swap(lax.dynamic_slice_in_dim(part, (1 - me) * width, width, 2), "pipe", 1)
    return lax.dynamic_slice_in_dim(part, me * width, width, 2).astype(F32) + sent.astype(F32)


def shifted(value, by):
    count = lax.axis_size("expert")
    return lax.ppermute(value, "expert", [(i, (i + by) % count) for i in range(count)])


def all_features(value):
    if lax.axis_size("pipe") != 2:
        return lax.all_gather(value, "pipe", axis=1, tiled=True)
    other = swap(value, "pipe", 1)
    return jnp.concatenate(in_order(value, other, lax.axis_index("pipe")), axis=1)


def deliver(chunks):
    groups = lax.axis_size("expert")
    width = chunks.shape[2] // lax.axis_size("pipe")
    start = lax.axis_index("pipe") * width
    moved = [shifted(lax.dynamic_slice_in_dim(chunks[s], start, width, 1), s) for s in range(1, groups)]
    return jnp.concatenate([chunks[0]] + [all_features(part) for part in moved], axis=0)


def on_device(tokens, expert_ids, gates, w_up, w_down, cotangent):
    groups = lax.axis_size("expert")
    me = lax.axis_index("expert")
    pairs, features, hidden_width = w_up.shape
    halves = 2 if pairs % 2 == 0 else 1
    sets = pairs // halves
    rows = groups * CAP
    own = tokens.shape[0]
    slots = -(-sets * CAP // 8) * 8

    place = jnp.arange(groups * sets, dtype=jnp.int32)
    wanted = ((lax.rem(place // sets + me, groups) * pairs + lax.rem(place, sets) * halves) // 2)[:, None]
    first, second = expert_ids[:, 0][None, :] == wanted, expert_ids[:, 1][None, :] == wanted
    chosen = first | second
    before = jnp.arange(own)[:, None] < jnp.arange(own)[None, :]
    position = jnp.dot(chosen.astype(BF), before.astype(BF), preferred_element_type=F32).astype(jnp.int32)
    slot = jnp.where(chosen, position + lax.rem(place, sets)[:, None] * CAP, -1)
    slot = slot.reshape(groups, sets, 1, own)
    column = jnp.arange(slots, dtype=jnp.int32)[None, None, :, None]
    match = slot == column
    routing = jnp.any(match, axis=1)
    gate = jnp.where(first, gates[:, 0][None, :], 0.0) + jnp.where(second, gates[:, 1][None, :], 0.0)
    weighting = jnp.sum(jnp.where(match, gate.reshape(groups, sets, 1, own), 0.0), axis=1)
    slot_weight = jnp.sum(weighting, axis=2)
    routing = routing.astype(BF)

    def spread(array):
        return jnp.einsum("gst,td->gsd", routing, array, preferred_element_type=F32)

    target = jnp.arange(pairs * rows, dtype=jnp.int32)
    inside = lax.rem(target, rows)
    source = (inside // CAP) * slots + (target // (rows * halves)) * CAP + lax.rem(inside, CAP)
    order = (source[:, None] == jnp.arange(groups * slots, dtype=jnp.int32)[None, :]).astype(BF)
    set_order = order.reshape(sets, halves, rows, groups * slots)[:, 0].reshape(sets * rows, groups * slots)

    def by_pair(arrivals):
        placed = jnp.dot(order, arrivals, preferred_element_type=F32).astype(BF)
        return placed.reshape(pairs, rows, features)

    arrivals = deliver(spread(tokens).astype(BF))
    grad_arrivals = deliver((spread(cotangent) * slot_weight[:, :, None]).astype(BF))
    arrived = by_pair(arrivals)
    pre_part = jnp.einsum("pcd,pdh->pch", arrived, w_up, preferred_element_type=F32).astype(BF)
    pre_near = near_sum(pre_part)
    grad_rows, pre_near = lax.optimization_barrier((by_pair(grad_arrivals), pre_near))
    pre_share = far_sum(pre_near)
    grad_part = jnp.einsum("pcd,phd->pch", grad_rows, w_down, preferred_element_type=F32).astype(BF)

    hidden = share_of_features(jax.nn.silu(pre_share).astype(BF), pairs)
    grad_share = far_sum(near_sum(grad_part))
    grad_pre = share_of_features((grad_share * silu_slope(pre_share)).astype(BF), pairs)

    def by_set(value):
        return value.reshape((sets, halves) + value.shape[1:])

    def back_to_tokens(summed):
        flat = summed.astype(BF).reshape(sets * rows, summed.shape[2])
        chunks = lax.dot_general(set_order, flat, (((0,), (0,)), ((), ())), preferred_element_type=F32)
        chunks = chunks.astype(BF).reshape(groups, slots, summed.shape[2])
        moved = [chunks[0]] + [shifted(chunks[s], groups - s) for s in range(1, groups)]
        return jnp.concatenate(moved, axis=0)

    out_part = jnp.einsum("rhck,rhkd->rcd", by_set(hidden), by_set(w_down), preferred_element_type=F32)
    out_home = back_to_tokens(sum_over_hidden(out_part))
    output = lax.dot_general(
        weighting.reshape(groups * slots, own), out_home.astype(F32),
        (((0,), (0,)), ((), ())), precision=lax.Precision.HIGHEST,
    ).astype(BF)
    down_grad = jnp.einsum("pch,pcd->phd", hidden, grad_rows, preferred_element_type=F32).astype(BF)
    grad_pre, down_grad = lax.optimization_barrier((grad_pre, down_grad))
    back_part = jnp.einsum("rhck,rhdk->rcd", by_set(grad_pre), by_set(w_up), preferred_element_type=F32)
    back_part, late = lax.optimization_barrier((back_part.astype(BF), grad_pre))
    back_home = back_to_tokens(sum_over_hidden(back_part))
    token_grad = lax.dot_general(
        routing.reshape(groups * slots, own), back_home, (((0,), (0,)), ((), ())),
        preferred_element_type=F32,
    ).astype(BF)
    up_grad = jnp.einsum("pcd,pch->pdh", arrived, late, preferred_element_type=F32).astype(BF)
    return (output, token_grad, up_grad, down_grad)


def solution(mesh):
    return jax.shard_map(
        on_device,
        mesh=mesh,
        in_specs=(
            P("expert", "dp"),
            P("expert", None),
            P("expert", None),
            P("expert", "dp", "pipe"),
            P("expert", "pipe", "dp"),
            P("expert", "dp"),
        ),
        out_specs=(
            P("expert", ("dp", "pipe")),
            P("expert", ("dp", "pipe")),
            P("expert", "dp", "pipe"),
            P("expert", "pipe", "dp"),
        ),
        check_vma=False,
    )
```

```python
import jax
import jax.numpy as jnp
from jax import lax
from jax.sharding import PartitionSpec as P

CAP = 34
BF = jnp.bfloat16
F32 = jnp.float32


def silu_slope(pre):
    sigma = jax.nn.sigmoid(pre)
    return sigma * (1.0 + pre * (1.0 - sigma))


def swap(value, axis, bit):
    count = lax.axis_size(axis)
    return lax.ppermute(value, axis, [(i, i ^ bit) for i in range(count)])


def pick(value, index, axis):
    return lax.dynamic_index_in_dim(value, index, axis, keepdims=False)


def near_sum(part):
    count = lax.axis_size("dp")
    pairs, rows, hidden = part.shape
    if count != 4 or pairs % 4:
        return part
    core = lax.axis_index("dp") % 2
    cut = part.reshape(2, 2, pairs // 4, rows, hidden)
    other = swap(pick(cut, 1 - core, 1), "dp", 1)
    return (pick(cut, core, 1).astype(F32) + other.astype(F32)).astype(BF)


def far_sum(near):
    if near.ndim == 3:
        return lax.psum_scatter(near, "dp", scatter_dimension=2, tiled=True).astype(F32)
    chip = lax.axis_index("dp") // 2
    far = swap(pick(near, 1 - chip, 0), "dp", 2)
    return pick(near, chip, 0).astype(F32) + far.astype(F32)


def in_order(mine, other, index):
    first = jnp.where(index == 0, mine, other)
    second = jnp.where(index == 0, other, mine)
    return first, second


def across(value, pairs):
    if lax.axis_size("dp") != 4 or pairs % 4:
        return value
    return swap(value, "dp", 2)


def share_of_features(value, far, pairs):
    if lax.axis_size("dp") != 4 or pairs % 4:
        return lax.all_gather(value, "dp", axis=2, tiled=True)
    me = lax.axis_index("dp")
    core, chip = me % 2, me // 2
    near = swap(value, "dp", 1)
    far_near = swap(far, "dp", 1)
    low, high = in_order(value, near, core)
    far_low, far_high = in_order(far, far_near, core)
    a0, a1 = in_order(low, far_low, chip)
    b0, b1 = in_order(high, far_high, chip)
    return jnp.concatenate([a0, b0, a1, b1], axis=0)


def sum_over_hidden(part):
    count = lax.axis_size("pipe")
    part = part.astype(BF)
    if count != 2:
        return lax.psum_scatter(part, "pipe", scatter_dimension=2, tiled=True).astype(F32)
    me = lax.axis_index("pipe")
    width = part.shape[2] // 2
    sent = swap(lax.dynamic_slice_in_dim(part, (1 - me) * width, width, 2), "pipe", 1)
    return lax.dynamic_slice_in_dim(part, me * width, width, 2).astype(F32) + sent.astype(F32)


def shifted(value, by):
    count = lax.axis_size("expert")
    return lax.ppermute(value, "expert", [(i, (i + by) % count) for i in range(count)])


def all_features(value):
    if lax.axis_size("pipe") != 2:
        return lax.all_gather(value, "pipe", axis=1, tiled=True)
    other = swap(value, "pipe", 1)
    return jnp.concatenate(in_order(value, other, lax.axis_index("pipe")), axis=1)


def send_out(chunks):
    groups = lax.axis_size("expert")
    width = chunks.shape[2] // lax.axis_size("pipe")
    start = lax.axis_index("pipe") * width
    return [shifted(lax.dynamic_slice_in_dim(chunks[s], start, width, 1), s) for s in range(1, groups)]


def in_full(chunks, moved):
    return jnp.concatenate([chunks[0]] + [all_features(part) for part in moved], axis=0)


def on_device(tokens, expert_ids, gates, w_up, w_down, cotangent):
    groups = lax.axis_size("expert")
    me = lax.axis_index("expert")
    pairs, features, hidden_width = w_up.shape
    halves = 2 if pairs % 2 == 0 else 1
    sets = pairs // halves
    rows = groups * CAP
    own = tokens.shape[0]
    slots = -(-sets * CAP // 8) * 8

    place = jnp.arange(groups * sets, dtype=jnp.int32)
    wanted = ((lax.rem(place // sets + me, groups) * pairs + lax.rem(place, sets) * halves) // 2)[:, None]
    first, second = expert_ids[:, 0][None, :] == wanted, expert_ids[:, 1][None, :] == wanted
    chosen = first | second
    before = jnp.arange(own)[:, None] < jnp.arange(own)[None, :]
    position = jnp.dot(chosen.astype(BF), before.astype(BF), preferred_element_type=F32).astype(jnp.int32)
    slot = jnp.where(chosen, position + lax.rem(place, sets)[:, None] * CAP, -1)
    slot = slot.reshape(groups, sets, 1, own)
    column = jnp.arange(slots, dtype=jnp.int32)[None, None, :, None]
    match = slot == column
    routing = jnp.any(match, axis=1)
    gate = jnp.where(first, gates[:, 0][None, :], 0.0) + jnp.where(second, gates[:, 1][None, :], 0.0)
    weighting = jnp.sum(jnp.where(match, gate.reshape(groups, sets, 1, own), 0.0), axis=1)
    slot_weight = jnp.sum(weighting, axis=2)
    routing = routing.astype(BF)

    def spread(array):
        return jnp.einsum("gst,td->gsd", routing, array, preferred_element_type=F32)

    target = jnp.arange(pairs * rows, dtype=jnp.int32)
    inside = lax.rem(target, rows)
    source = (inside // CAP) * slots + (target // (rows * halves)) * CAP + lax.rem(inside, CAP)
    order = (source[:, None] == jnp.arange(groups * slots, dtype=jnp.int32)[None, :]).astype(BF)
    set_order = order.reshape(sets, halves, rows, groups * slots)[:, 0].reshape(sets * rows, groups * slots)

    def by_pair(arrivals):
        placed = jnp.dot(order, arrivals, preferred_element_type=F32).astype(BF)
        return placed.reshape(pairs, rows, features)

    chunks = spread(tokens).astype(BF)
    moved, late_cotangent = lax.optimization_barrier((send_out(chunks), cotangent))
    grad_chunks = (spread(late_cotangent) * slot_weight[:, :, None]).astype(BF)
    grad_moved = send_out(grad_chunks)
    arrived = by_pair(in_full(chunks, moved))
    pre_part = jnp.einsum("pcd,pdh->pch", arrived, w_up, preferred_element_type=F32).astype(BF)
    pre_part, grad_arrivals = lax.optimization_barrier((pre_part, in_full(grad_chunks, grad_moved)))
    grad_rows, pre_near = lax.optimization_barrier((by_pair(grad_arrivals), near_sum(pre_part)))
    pre_share = far_sum(pre_near)
    grad_part = jnp.einsum("pcd,phd->pch", grad_rows, w_down, preferred_element_type=F32).astype(BF)
    hidden_share = jax.nn.silu(pre_share).astype(BF)
    grad_part, pre_share, hidden_share = lax.optimization_barrier((grad_part, pre_share, hidden_share))
    grad_near, hidden_far = lax.optimization_barrier((near_sum(grad_part), across(hidden_share, pairs)))
    hidden = share_of_features(hidden_share, hidden_far, pairs)
    grad_share = far_sum(grad_near)

    def by_set(value):
        return value.reshape((sets, halves) + value.shape[1:])

    def back_to_tokens(summed):
        flat = summed.astype(BF).reshape(sets * rows, summed.shape[2])
        chunks = lax.dot_general(set_order, flat, (((0,), (0,)), ((), ())), preferred_element_type=F32)
        chunks = chunks.astype(BF).reshape(groups, slots, summed.shape[2])
        moved = [chunks[0]] + [shifted(chunks[s], groups - s) for s in range(1, groups)]
        return jnp.concatenate(moved, axis=0)

    out_part = jnp.einsum("rhck,rhkd->rcd", by_set(hidden), by_set(w_down), preferred_element_type=F32)
    out_part, late_hidden, grad_share = lax.optimization_barrier((out_part.astype(BF), hidden, grad_share))
    grad_pre_share = (grad_share * silu_slope(pre_share)).astype(BF)
    grad_pre = share_of_features(grad_pre_share, across(grad_pre_share, pairs), pairs)
    down_grad = jnp.einsum("pch,pcd->phd", late_hidden, grad_rows, preferred_element_type=F32).astype(BF)
    grad_pre, down_grad, out_rows = lax.optimization_barrier(
        (grad_pre, down_grad, sum_over_hidden(out_part))
    )
    out_home = back_to_tokens(out_rows)
    back_part = jnp.einsum("rhck,rhdk->rcd", by_set(grad_pre), by_set(w_up), preferred_element_type=F32)
    back_part, late_grad_pre, out_home = lax.optimization_barrier(
        (back_part.astype(BF), grad_pre, out_home)
    )
    up_grad = jnp.einsum("pcd,pch->pdh", arrived, late_grad_pre, preferred_element_type=F32).astype(BF)
    output = lax.dot_general(
        weighting.reshape(groups * slots, own), out_home.astype(F32),
        (((0,), (0,)), ((), ())), precision=lax.Precision.HIGHEST,
    ).astype(BF)
    back_rows, up_grad, output = lax.optimization_barrier((sum_over_hidden(back_part), up_grad, output))
    back_home = back_to_tokens(back_rows)
    token_grad = lax.dot_general(
        routing.reshape(groups * slots, own), back_home, (((0,), (0,)), ((), ())),
        preferred_element_type=F32,
    ).astype(BF)
    return (output, token_grad, up_grad, down_grad)


def solution(mesh):
    return jax.shard_map(
        on_device,
        mesh=mesh,
        in_specs=(
            P("expert", "dp"),
            P("expert", None),
            P("expert", None),
            P("expert", "dp", "pipe"),
            P("expert", "pipe", "dp"),
            P("expert", "dp"),
        ),
        out_specs=(
            P("expert", ("dp", "pipe")),
            P("expert", ("dp", "pipe")),
            P("expert", "dp", "pipe"),
            P("expert", "pipe", "dp"),
        ),
        check_vma=False,
    )
```

```python
import jax
import jax.numpy as jnp
from jax import lax
from jax.sharding import PartitionSpec as P

CAP = 34
BF = jnp.bfloat16
F32 = jnp.float32


def silu_slope(pre):
    sigma = jax.nn.sigmoid(pre)
    return sigma * (1.0 + pre * (1.0 - sigma))


def swap(value, axis, bit):
    count = lax.axis_size(axis)
    return lax.ppermute(value, axis, [(i, i ^ bit) for i in range(count)])


def pick(value, index, axis):
    return lax.dynamic_index_in_dim(value, index, axis, keepdims=False)


def near_sum(part):
    count = lax.axis_size("dp")
    pairs, rows, hidden = part.shape
    if count != 4 or pairs % 4:
        return part
    core = lax.axis_index("dp") % 2
    cut = part.reshape(2, 2, pairs // 4, rows, hidden)
    other = swap(pick(cut, 1 - core, 1), "dp", 1)
    return (pick(cut, core, 1).astype(F32) + other.astype(F32)).astype(BF)


def far_sum(near):
    if near.ndim == 3:
        return lax.psum_scatter(near, "dp", scatter_dimension=2, tiled=True).astype(F32)
    chip = lax.axis_index("dp") // 2
    far = swap(pick(near, 1 - chip, 0), "dp", 2)
    return pick(near, chip, 0).astype(F32) + far.astype(F32)


def in_order(mine, other, index):
    first = jnp.where(index == 0, mine, other)
    second = jnp.where(index == 0, other, mine)
    return first, second


def across(value, pairs):
    if lax.axis_size("dp") != 4 or pairs % 4:
        return value
    return swap(value, "dp", 2)


def share_of_features(value, far, pairs):
    if lax.axis_size("dp") != 4 or pairs % 4:
        return lax.all_gather(value, "dp", axis=2, tiled=True)
    me = lax.axis_index("dp")
    core, chip = me % 2, me // 2
    near = swap(value, "dp", 1)
    far_near = swap(far, "dp", 1)
    low, high = in_order(value, near, core)
    far_low, far_high = in_order(far, far_near, core)
    a0, a1 = in_order(low, far_low, chip)
    b0, b1 = in_order(high, far_high, chip)
    return jnp.concatenate([a0, b0, a1, b1], axis=0)


def sum_over_hidden(part):
    count = lax.axis_size("pipe")
    part = part.astype(BF)
    if count != 2:
        return lax.psum_scatter(part, "pipe", scatter_dimension=2, tiled=True).astype(F32)
    me = lax.axis_index("pipe")
    width = part.shape[2] // 2
    sent = swap(lax.dynamic_slice_in_dim(part, (1 - me) * width, width, 2), "pipe", 1)
    return lax.dynamic_slice_in_dim(part, me * width, width, 2).astype(F32) + sent.astype(F32)


def shifted(value, by):
    count = lax.axis_size("expert")
    return lax.ppermute(value, "expert", [(i, (i + by) % count) for i in range(count)])


def all_features(value):
    if lax.axis_size("pipe") != 2:
        return lax.all_gather(value, "pipe", axis=1, tiled=True)
    other = swap(value, "pipe", 1)
    return jnp.concatenate(in_order(value, other, lax.axis_index("pipe")), axis=1)


def send_out(chunks):
    groups = lax.axis_size("expert")
    width = chunks.shape[2] // lax.axis_size("pipe")
    start = lax.axis_index("pipe") * width
    return [shifted(lax.dynamic_slice_in_dim(chunks[s], start, width, 1), s) for s in range(1, groups)]


def in_full(chunks, moved):
    return jnp.concatenate([chunks[0]] + [all_features(part) for part in moved], axis=0)


def on_device(tokens, expert_ids, gates, w_up, w_down, cotangent):
    groups = lax.axis_size("expert")
    me = lax.axis_index("expert")
    pairs, features, hidden_width = w_up.shape
    halves = 2 if pairs % 2 == 0 else 1
    sets = pairs // halves
    rows = groups * CAP
    own = tokens.shape[0]
    slots = -(-sets * CAP // 8) * 8

    place = jnp.arange(groups * sets, dtype=jnp.int32)
    wanted = ((lax.rem(place // sets + me, groups) * pairs + lax.rem(place, sets) * halves) // 2)[:, None]
    first, second = expert_ids[:, 0][None, :] == wanted, expert_ids[:, 1][None, :] == wanted
    chosen = first | second
    before = jnp.arange(own)[:, None] < jnp.arange(own)[None, :]
    position = jnp.dot(chosen.astype(BF), before.astype(BF), preferred_element_type=F32).astype(jnp.int32)
    slot = jnp.where(chosen, position + lax.rem(place, sets)[:, None] * CAP, -1)
    slot = slot.reshape(groups, sets, 1, own)
    column = jnp.arange(slots, dtype=jnp.int32)[None, None, :, None]
    match = slot == column
    routing = jnp.any(match, axis=1)
    gate = jnp.where(first, gates[:, 0][None, :], 0.0) + jnp.where(second, gates[:, 1][None, :], 0.0)
    weighting = jnp.sum(jnp.where(match, gate.reshape(groups, sets, 1, own), 0.0), axis=1)
    slot_weight = jnp.sum(weighting, axis=2)
    routing = routing.astype(BF)

    def spread(array):
        return jnp.einsum("gst,td->gsd", routing, array, preferred_element_type=F32)

    target = jnp.arange(pairs * rows, dtype=jnp.int32)
    inside = lax.rem(target, rows)
    source = (inside // CAP) * slots + (target // (rows * halves)) * CAP + lax.rem(inside, CAP)
    order = (source[:, None] == jnp.arange(groups * slots, dtype=jnp.int32)[None, :]).astype(BF)
    set_order = order.reshape(sets, halves, rows, groups * slots)[:, 0].reshape(sets * rows, groups * slots)

    def by_pair(arrivals):
        placed = jnp.dot(order, arrivals, preferred_element_type=F32).astype(BF)
        return placed.reshape(pairs, rows, features)

    chunks = spread(tokens).astype(BF)
    moved, late_cotangent = lax.optimization_barrier((send_out(chunks), cotangent))
    grad_chunks = (spread(late_cotangent) * slot_weight[:, :, None]).astype(BF)
    grad_moved = send_out(grad_chunks)
    arrived = by_pair(in_full(chunks, moved))
    pre_part = jnp.einsum("pcd,pdh->pch", arrived, w_up, preferred_element_type=F32).astype(BF)
    pre_part, grad_arrivals = lax.optimization_barrier((pre_part, in_full(grad_chunks, grad_moved)))
    grad_rows, pre_near = lax.optimization_barrier((by_pair(grad_arrivals), near_sum(pre_part)))
    pre_share = far_sum(pre_near)
    grad_part = jnp.einsum("pcd,phd->pch", grad_rows, w_down, preferred_element_type=F32).astype(BF)
    hidden_share = jax.nn.silu(pre_share).astype(BF)
    grad_part, pre_share, hidden_share = lax.optimization_barrier((grad_part, pre_share, hidden_share))
    grad_near, hidden_far = lax.optimization_barrier((near_sum(grad_part), across(hidden_share, pairs)))
    hidden = share_of_features(hidden_share, hidden_far, pairs)
    grad_share = far_sum(grad_near)

    def by_set(value):
        return value.reshape((sets, halves) + value.shape[1:])

    def back_to_tokens(summed):
        flat = summed.astype(BF).reshape(sets * rows, summed.shape[2])
        chunks = lax.dot_general(set_order, flat, (((0,), (0,)), ((), ())), preferred_element_type=F32)
        chunks = chunks.astype(BF).reshape(groups, slots, summed.shape[2])
        moved = [chunks[0]] + [shifted(chunks[s], groups - s) for s in range(1, groups)]
        return jnp.concatenate(moved, axis=0)

    out_part = jnp.einsum("rhck,rhkd->rcd", by_set(hidden), by_set(w_down), preferred_element_type=F32)
    out_part, late_hidden, grad_share = lax.optimization_barrier((out_part.astype(BF), hidden, grad_share))
    grad_pre_share = (grad_share * silu_slope(pre_share)).astype(BF)
    grad_pre_far = across(grad_pre_share, pairs)
    down_grad = jnp.einsum("pch,pcd->phd", late_hidden, grad_rows, preferred_element_type=F32).astype(BF)
    grad_pre_far, down_grad, out_rows = lax.optimization_barrier(
        (grad_pre_far, down_grad, sum_over_hidden(out_part))
    )
    grad_pre = share_of_features(grad_pre_share, grad_pre_far, pairs)
    grad_pre, out_rows = lax.optimization_barrier((grad_pre, out_rows))
    out_home = back_to_tokens(out_rows)
    back_part = jnp.einsum("rhck,rhdk->rcd", by_set(grad_pre), by_set(w_up), preferred_element_type=F32)
    back_part, late_grad_pre, out_home = lax.optimization_barrier(
        (back_part.astype(BF), grad_pre, out_home)
    )
    up_grad = jnp.einsum("pcd,pch->pdh", arrived, late_grad_pre, preferred_element_type=F32).astype(BF)
    output = lax.dot_general(
        weighting.reshape(groups * slots, own), out_home.astype(F32),
        (((0,), (0,)), ((), ())), precision=lax.Precision.HIGHEST,
    ).astype(BF)
    back_rows, up_grad, output = lax.optimization_barrier((sum_over_hidden(back_part), up_grad, output))
    back_home = back_to_tokens(back_rows)
    token_grad = lax.dot_general(
        routing.reshape(groups * slots, own), back_home, (((0,), (0,)), ((), ())),
        preferred_element_type=F32,
    ).astype(BF)
    return (output, token_grad, up_grad, down_grad)


def solution(mesh):
    return jax.shard_map(
        on_device,
        mesh=mesh,
        in_specs=(
            P("expert", "dp"),
            P("expert", None),
            P("expert", None),
            P("expert", "dp", "pipe"),
            P("expert", "pipe", "dp"),
            P("expert", "dp"),
        ),
        out_specs=(
            P("expert", ("dp", "pipe")),
            P("expert", ("dp", "pipe")),
            P("expert", "dp", "pipe"),
            P("expert", "pipe", "dp"),
        ),
        check_vma=False,
    )
```
